512 devices in a mesh: frame: 16 (over x, z_hi, core), space: 32 (over z_lo, y).
Axes of the slice: x: 4, y: 4, z: 16 (z_hi: 2, z_lo: 8; z = z_hi * 8 + z_lo), core: 2. Of those that a mesh axis runs over, the one named last changes fastest.
Arguments:
- q_space: bfloat16 [32, 2048, 1536], P('frame', 'space'), may hold values from -28 to 28
- k_space: bfloat16 [32, 2048, 1536], P('frame', 'space'), may hold values from -28 to 28
- v_space: bfloat16 [32, 2048, 1536], P('frame', 'space'), may hold values from -6 to 6
- q_time: bfloat16 [32, 2048, 1536], P('frame', 'space'), may hold values from -28 to 28
- k_time: bfloat16 [32, 2048, 1536], P('frame', 'space'), may hold values from -28 to 28
- v_time: bfloat16 [32, 2048, 1536], P('frame', 'space'), may hold values from -6 to 6
- out_grad: bfloat16 [32, 2048, 1536], P('frame', 'space'), may hold values from -6 to 6
- key_gain_space: float32 [1536], replicated, may hold values from 0.25 to 1.75
- value_gain_space: float32 [1536], replicated, may hold values from 0.25 to 1.75
- key_gain_time: float32 [1536], replicated, may hold values from 0.25 to 1.75
- value_gain_time: float32 [1536], replicated, may hold values from 0.25 to 1.75
Outputs:
- q_grad_space: bfloat16 [32, 2048, 1536], P('frame', 'space')
- k_grad_space: bfloat16 [32, 2048, 1536], P('frame', 'space')
- v_grad_space: bfloat16 [32, 2048, 1536], P('frame', 'space')
- q_grad_time: bfloat16 [32, 2048, 1536], P('frame', 'space')
- k_grad_time: bfloat16 [32, 2048, 1536], P('frame', 'space')
- v_grad_time: bfloat16 [32, 2048, 1536], P('frame', 'space')
- ia3_grads: float32 [4, 1536], replicated
The draws below stay inside these ranges and needn't reach their ends.
All inputs are finite; a program needn't handle non-finite values.
Results may differ from the reference program's by a relative error of at most 0.003.
The reference program's roundings to bfloat16 on the way count: a program that leaves them out, or rounds other values in their place, can miss the bound.
Values may be sent and summed in bfloat16 or wider, within the bound.
A program may use at most 64 MiB of HBM per device.

```python
import jax
import jax.numpy as jnp
from jax import lax

H = 16
HD = 96
D = 1536
F = 32
S = 2048
TOKENS = 65536


def align_rows(key, seq_axis):
    key = jax.random.fold_in(key, 40 + seq_axis)
    keys_all = jax.random.split(key, 2)
    shape = (F, S, D)
    query_matrix = jnp.clip(jax.random.normal(keys_all[0], shape, jnp.float32), -6.0, 6.0)
    key_matrix = jnp.clip(jax.random.normal(keys_all[1], shape, jnp.float32), -6.0, 6.0)
    return (query_matrix, key_matrix)


def draw_q_space(key, part):
    return align_rows(key, 1)[0].astype(jnp.bfloat16)


def draw_k_space(key, part):
    return align_rows(key, 1)[1].astype(jnp.bfloat16)


def draw_q_time(key, part):
    return align_rows(key, 0)[0].astype(jnp.bfloat16)


def draw_k_time(key, part):
    return align_rows(key, 0)[1].astype(jnp.bfloat16)


def block_scale(own_key, extent, cuts, least, high):
    def one(axis_at, shards_of):
        draws = jax.random.uniform(jax.random.fold_in(jax.random.fold_in(own_key, 6), axis_at), (shards_of,), jnp.float32, least / len(cuts), high / len(cuts))
        return jnp.repeat(jnp.exp(draws), extent[axis_at] // shards_of).reshape((-1,) + (1,) * (len(extent) - axis_at - 1))

    loudness = one(*cuts[0])
    for cut in cuts[1:]:
        loudness = loudness * one(*cut)
    return loudness


def normal_values(own_key, dims, width, bound, shards=(), dtype=jnp.bfloat16):
    values = jax.random.normal(own_key, dims, jnp.float32) * width
    if len(shards) > 0:
        values = block_scale(own_key, dims, shards, -0.22, 0.18) * values
    return jnp.clip(values, min=-bound, max=bound).astype(dtype)


def setup_inputs(seed: int = 0) -> dict:
    arg_keys = jax.random.split(jax.random.key(seed), 12)
    return {
        "q_space": draw_q_space(jax.random.fold_in(arg_keys[11], 71), 0),
        "k_space": draw_k_space(jax.random.fold_in(arg_keys[11], 71), 0),
        "v_space": normal_values(arg_keys[2], (F, S, D), 1.0, 6.0, ((0, 16), (1, 32))),
        "q_time": draw_q_time(jax.random.fold_in(arg_keys[11], 71), 0),
        "k_time": draw_k_time(jax.random.fold_in(arg_keys[11], 71), 0),
        "v_time": normal_values(arg_keys[5], (F, S, D), 1.0, 6.0, ((0, 16), (1, 32))),
        "out_grad": normal_values(arg_keys[6], (F, S, D), 1.0, 6.0, ((0, 16), (1, 32))),
        "key_gain_space": jnp.clip(1.0 + 0.15 * jax.random.normal(arg_keys[7], (D,), jnp.float32), 0.25, 1.75),
        "value_gain_space": jnp.clip(1.0 + 0.15 * jax.random.normal(arg_keys[8], (D,), jnp.float32), 0.25, 1.75),
        "key_gain_time": jnp.clip(1.0 + 0.15 * jax.random.normal(arg_keys[9], (D,), jnp.float32), 0.25, 1.75),
        "value_gain_time": jnp.clip(1.0 + 0.15 * jax.random.normal(arg_keys[10], (D,), jnp.float32), 0.25, 1.75),
    }


def core_backward(members):
    query_matrix, key_matrix, value_matrix, gradient_lines = [member.astype(jnp.float32) for member in members]
    logit_scale = query_matrix.shape[-1] ** -0.5
    score_matrix = jnp.einsum('jkz,ikz->kji', query_matrix, key_matrix) * logit_scale
    row_max = jnp.max(score_matrix, axis=-1, keepdims=True)
    exp_terms = jnp.exp(score_matrix - row_max)
    probs_f = exp_terms / jnp.sum(exp_terms, axis=-1, keepdims=True)
    probabilities_narrow = lax.optimization_barrier(probs_f.astype(jnp.bfloat16)).astype(jnp.float32)
    value_gradient = jnp.einsum('xny,nxe->yxe', probabilities_narrow, gradient_lines).astype(jnp.bfloat16)
    probability_gradient = jnp.einsum('jkz,ikz->kji', gradient_lines, value_matrix)
    row_delta = jnp.sum(probs_f * probability_gradient, axis=-1, keepdims=True)
    score_gradient = (probs_f * (probability_gradient - row_delta) * logit_scale).astype(jnp.bfloat16)
    score_gradient = lax.optimization_barrier(score_gradient).astype(jnp.float32)
    query_gradient = jnp.einsum('jzx,xjy->zjy', score_gradient, key_matrix).astype(jnp.bfloat16)
    key_gradient = jnp.einsum('xny,nxe->yxe', score_gradient, query_matrix).astype(jnp.bfloat16)
    return query_gradient, key_gradient, value_gradient


def scaled(tensor, gain):
    return (tensor.astype(jnp.float32) * gain).astype(jnp.bfloat16)


def attention_grads(query_matrix, key_matrix, value_matrix, out_grad, key_gain, value_gain, temporal):
    key_scaled = scaled(key_matrix, key_gain)
    value_scaled = scaled(value_matrix, value_gain)
    split_shape = (F, S, H, HD)
    members = [member.reshape(split_shape) for member in (query_matrix, key_scaled, value_scaled, out_grad)]
    if temporal:
        members = [jnp.swapaxes(member, 0, 1) for member in members]
    query_gradient, key_gradient, value_gradient = lax.map(core_backward, tuple(members))
    if temporal:
        query_gradient = jnp.swapaxes(query_gradient, 0, 1)
        key_gradient = jnp.swapaxes(key_gradient, 0, 1)
        value_gradient = jnp.swapaxes(value_gradient, 0, 1)
    query_gradient = query_gradient.reshape(F, S, D)
    key_gradient = key_gradient.reshape(F, S, D)
    value_gradient = value_gradient.reshape(F, S, D)
    key_term = jnp.sum(key_gradient.astype(jnp.float32) * key_matrix.astype(jnp.float32), axis=(0, 1))
    value_term = jnp.sum(value_gradient.astype(jnp.float32) * value_matrix.astype(jnp.float32), axis=(0, 1))
    return query_gradient, scaled(key_gradient, key_gain), scaled(value_gradient, value_gain), key_term, value_term


def reference(q_space, k_space, v_space, q_time, k_time, v_time, out_grad, key_gain_space, value_gain_space, key_gain_time, value_gain_time):
    space_q, space_k, space_v, space_kt, space_vt = attention_grads(q_space, k_space, v_space, out_grad, key_gain_space, value_gain_space, False)
    time_q, time_k, time_v, time_kt, time_vt = attention_grads(q_time, k_time, v_time, out_grad, key_gain_time, value_gain_time, True)
    norm_factor = float(TOKENS) ** -0.5
    ia3_grads = jnp.stack([space_kt, space_vt, time_kt, time_vt]) * norm_factor
    return space_q, space_k, space_v, time_q, time_k, time_v, ia3_grads
```

```python
import functools

import jax
import jax.numpy as jnp
from jax import lax
from jax.experimental import pallas as pl
from jax.experimental.pallas import tpu as pltpu
from jax.sharding import PartitionSpec as P

F32, BF16 = jnp.float32, jnp.bfloat16
H = 16
HD = 96
NS = 32
NF = 16
FL = 2
PL = 64
SEQ = NS * PL
ROWS = PL * HD // 128
SPAN = 512
QB = 256
KT = 256
SCALE = HD**-0.5
LOG2E = 1.4426950408889634
NT = (((1,), (1,)), ((), ()))
NN = (((1,), (0,)), ((), ()))
MESH = pl.DeviceIdType.MESH


def mm(a, b, dims):
    return lax.dot_general(a, b, dims, preferred_element_type=F32)


def lanes(shape):
    return lax.broadcasted_iota(jnp.int32, shape, len(shape) - 1)


def split_heads(x):
    a, b, c = x[:, 0:128], x[:, 128:256], x[:, 256:384]
    lane = lanes(a.shape)
    return (
        a,
        jnp.where(lane < 32, pltpu.roll(a, 32, 1), pltpu.roll(b, 32, 1)),
        jnp.where(lane < 64, pltpu.roll(b, 64, 1), pltpu.roll(c, 64, 1)),
        pltpu.roll(c, 96, 1),
    )


def join_heads(w, x, y, z):
    lane = lanes(w.shape)
    x, y, z = pltpu.roll(x, 96, 1), pltpu.roll(y, 64, 1), pltpu.roll(z, 32, 1)
    return jnp.where(lane < 96, w, x), jnp.where(lane < 64, x, y), jnp.where(lane < 32, y, z)


def pack_tiles(t0, t1, t2, t3):
    lane = lanes(t0.shape)
    return (
        jnp.where(lane < 96, t0, pltpu.roll(t3, 96, 1)),
        jnp.where(lane < 96, t1, pltpu.roll(t3, 64, 1)),
        jnp.where(lane < 96, t2, pltpu.roll(t3, 32, 1)),
    )


def unpack_tiles(p0, p1, p2):
    lane = lanes(p0.shape)
    zero = jnp.zeros_like(p0)
    last = jnp.where(lane < 32, pltpu.roll(p0, 32, 1), pltpu.roll(p1, 64, 1))
    last = jnp.where(lane < 64, last, pltpu.roll(p2, 96, 1))
    return tuple(jnp.where(lane < 96, t, zero) for t in (p0, p1, p2, last))


def tiles_of(ref, lead, count=3):
    return [ref[(*lead, pl.ds(16 * t, 16), slice(None))] for t in range(count)]


def attend(q, ks, vs, g, kt, dq, dk, dv, s_scr, p_scr, span, masked):
    tiles = span // KT
    for c in range(SEQ // 128):
        kt[:, c * 128 : (c + 1) * 128] = ks[c * 128 : (c + 1) * 128, :].T
    dk[...] = jnp.zeros_like(dk)
    dv[...] = jnp.zeros_like(dv)

    def step(start, base):
        rows = pl.ds(pl.multiple_of(start, QB), QB)
        keys = [pl.ds(pl.multiple_of(base + t * KT, KT), KT) for t in range(tiles)]
        tile = [pl.ds(t * KT, KT) for t in range(tiles)]
        qi, gi = q[rows, :], g[rows, :]
        if masked:
            key_pos = lax.broadcasted_iota(jnp.int32, (KT, QB), 0) & 15
            same = key_pos == (lanes((KT, QB)) & 15)
        top = None
        for t in range(tiles):
            s = mm(ks[keys[t], :], qi, NT)
            if masked:
                s = jnp.where(same, s, -jnp.inf)
            s_scr[tile[t], :] = s
            here = jnp.max(s.reshape(KT // 8, 8, QB), axis=0)
            top = here if top is None else jnp.maximum(top, here)
        top = jnp.max(top, axis=0, keepdims=True)
        total = jnp.zeros((8, QB), F32)
        delta = jnp.zeros((8, QB), F32)
        for t in range(tiles):
            e = jnp.exp2((s_scr[tile[t], :] - top) * (SCALE * LOG2E))
            dp = mm(vs[keys[t], :], gi, NT)
            s_scr[tile[t], :] = e
            p_scr[tile[t], :] = dp
            total += jnp.sum(e.reshape(KT // 8, 8, QB), axis=0)
            delta += jnp.sum((e * dp).reshape(KT // 8, 8, QB), axis=0)
        inv = 1.0 / jnp.sum(total, axis=0, keepdims=True)
        delta = jnp.sum(delta, axis=0, keepdims=True) * inv
        dq_t = jnp.zeros((HD, QB), F32)
        for t in range(tiles):
            p = s_scr[tile[t], :] * inv
            ds = (p * (p_scr[tile[t], :] - delta) * SCALE).astype(BF16)
            dv[keys[t], :] += mm(p.astype(BF16), gi, NN)
            dk[keys[t], :] += mm(ds, qi, NN)
            dq_t += mm(kt[0:HD, keys[t]], ds, NN)
        dq[rows, 0:HD] = dq_t.T.astype(BF16)

    def outer(b, carry):
        for i in range(span // QB if masked else 1):
            step(b * (span if masked else QB) + i * QB, b * span if masked else 0)
        return carry

    lax.fori_loop(0, SEQ // (span if masked else QB), outer, 0)


def kernel(
    q_s, k_s, v_s, q_t, k_t, v_t, grad, gain_ks, gain_vs, gain_kt, gain_vt,
    dq_s, dk_s, dv_s, dq_t, dk_t, dv_t, ia3,
    s_out, s_in, t_out, t_in, sb_out, sb_in, tb_out, tb_in,
    q, k, v, ks, vs, g, kt, dq, dk, dv, s_scr, p_scr, gains,
    a_out, as1, at1, as2, at2,
    send_sem, s_sem, t_sem, sb_sem, tb_sem, a_send, as1_sem, at1_sem, as2_sem, at2_sem,
):
    f = lax.axis_index("frame")
    s = lax.axis_index("space")
    z, y = s // 4, s % 4
    fx, fz, fc = f // 4, (f // 2) % 2, f % 2

    def space_id(i):
        zi, yi = i // 4, i % 4
        half = (z // 4 + 1 + zi // 4) % 2
        return (4 * half + (z + zi) % 4) * 4 + (y + yi) % 4

    def space_z(i):
        half = (z // 4 + 1 + i // 4) % 2
        return 4 * half + (z + i) % 4

    def frame_id(i):
        zi = (fz + 1 + i // 8) % 2
        return 4 * ((fx + i // 2) % 4) + 2 * zi + (fc + i) % 2

    def send(axis, me, to, src, dst, ssem, rsem):
        @pl.when(to != me)
        def _():
            pltpu.make_async_remote_copy(
                src.at[to], dst.at[me], ssem, rsem.at[me], device_id={axis: to}, device_id_type=MESH
            ).start()

        @pl.when(to == me)
        def _():
            pltpu.make_async_copy(src.at[me], dst.at[me], rsem.at[me]).start()

    def arrived(dst, rsem, j):
        pltpu.make_async_copy(dst.at[j], dst.at[j], rsem.at[j]).wait()

    def sent(src, n, sem):
        part = src.at[pl.ds(0, n - 1)]
        pltpu.make_async_copy(part, part, sem).wait()

    def loop(n, body):
        def run(i, carry):
            body(i)
            return carry

        lax.fori_loop(0, n, run, 0)

    barrier = pltpu.get_barrier_semaphore()

    def greet(axis, me, n):
        def body(i):
            pl.semaphore_signal(
                barrier, inc=1, device_id={axis: (me + 1 + i) % n}, device_id_type=MESH
            )

        loop(n - 1, body)

    greet("space", s, NS)
    greet("frame", f, NF)

    def gain_body(i):
        cols = pl.ds(pl.multiple_of(i * 384, 128), 384)
        for r, ref in enumerate((gain_ks, gain_vs, gain_kt, gain_vt)):
            heads = split_heads(jnp.broadcast_to(ref[:, cols], (8, 384)))
            for j in range(4):
                gains[r, 4 * i + j] = heads[j]

    loop(H // 4, gain_body)

    def pack_group(ref, fl, hg):
        cols = pl.ds(pl.multiple_of(hg * 384, 128), 384)
        heads = split_heads(ref[fl, :, cols])
        return [pack_tiles(*(x[16 * t : 16 * t + 16] for t in range(4))) for x in heads]

    def put(ref, lead, tiles):
        for t in range(3):
            ref[(*lead, pl.ds(16 * t, 16), slice(None))] = tiles[t]

    pl.semaphore_wait(barrier, NS + NF - 2)

    def space_pack(i):
        zi = space_z(i)
        fl, hg = zi // 4, zi % 4
        for n, ref in enumerate((q_s, k_s, v_s, grad)):
            packed = pack_group(ref, fl, hg)
            for j in range(4):
                put(s_out, (4 * zi + j, n), packed[j])
                if n == 3:
                    put(t_out, (4 * hg + j, fl, n), packed[j])
        for j in range(4):
            send("space", s, 4 * zi + (y + j) % 4, s_out, s_in, send_sem.at[0], s_sem)

    loop(8, space_pack)

    def time_pack(i):
        fl, hg = i // 4, i % 4
        for n, ref in enumerate((q_t, k_t, v_t)):
            packed = pack_group(ref, fl, hg)
            for j in range(4):
                put(t_out, (4 * hg + j, fl, n), packed[j])

    loop(8, time_pack)
    loop(NF, lambda i: send("frame", f, frame_id(i), t_out, t_in, send_sem.at[1], t_sem))

    def unpack_item(ref, lead, row_of, gain_k, gain_v):
        for n, dst in enumerate((q, k, v, g)):
            tiles = unpack_tiles(*tiles_of(ref, (*lead, n)))
            for t in range(4):
                rows = pl.ds(pl.multiple_of(row_of(t), 16), 16)
                dst[rows, :] = tiles[t]
                if n == 1:
                    ks[rows, :] = (tiles[t].astype(F32) * gain_k).astype(BF16)
                if n == 2:
                    vs[rows, :] = (tiles[t].astype(F32) * gain_v).astype(BF16)

    def pack_item(ref, lead, row_of, gain_k, gain_v):
        for n, src in enumerate((dq, dk, dv)):
            tiles = []
            for t in range(4):
                x = src[pl.ds(pl.multiple_of(row_of(t), 16), 16), :]
                if n:
                    gain = gain_k if n == 1 else gain_v
                    x = (x.astype(BF16).astype(F32) * gain).astype(BF16)
                tiles.append(x)
            put(ref, (*lead, n), pack_tiles(*tiles))

    def gain_rows(row, head):
        return gains[row, head, 0:1, :], gains[row + 1, head, 0:1, :]

    def terms(slot):
        def body(i, carry):
            rows = pl.ds(pl.multiple_of(i * 128, 128), 128)
            out = []
            for acc, a, b in ((carry[0], dk, k), (carry[1], dv, v)):
                prod = a[rows, :].astype(BF16).astype(F32) * b[rows, :].astype(F32)
                out.append(acc + jnp.sum(prod.reshape(16, 8, 128), axis=0))
            return tuple(out)

        zero = jnp.zeros((8, 128), F32)
        tk, tv = lax.fori_loop(0, SEQ // 128, body, (zero, zero))
        a_out[slot] = jnp.concatenate(
            [jnp.sum(tk, axis=0, keepdims=True), jnp.sum(tv, axis=0, keepdims=True), zero[2:]]
        )

    def share(axis, me, n, slot, dst, rsem):
        dst[me] = a_out[slot]

        def body(i):
            pltpu.make_async_remote_copy(
                a_out.at[slot],
                dst.at[me],
                a_send.at[slot],
                rsem.at[me],
                device_id={axis: (me + 1 + i) % n},
                device_id_type=MESH,
            ).start()

        loop(n - 1, body)

    def collect(me, n, dst, rsem):
        loop(n - 1, lambda i: arrived(dst, rsem, (me + 1 + i) % n))

    head = s % H
    gk, gv = gain_rows(0, head)

    def space_unpack(i):
        j = space_id(i)
        arrived(s_in, s_sem, j)
        unpack_item(s_in, (j,), lambda t: PL * j + 16 * t, gk, gv)

    loop(NS, space_unpack)
    dq[...] = jnp.zeros_like(dq)
    attend(q, ks, vs, g, kt, dq, dk, dv, s_scr, p_scr, SEQ, False)

    def space_back(i):
        j = space_id(i)
        pack_item(sb_out, (j,), lambda t: PL * j + 16 * t, gk, gv)
        send("space", s, j, sb_out, sb_in, send_sem.at[2], sb_sem)

    loop(NS, space_back)
    terms(0)
    share("frame", f, NF, 0, as1, as1_sem)

    gk2, gv2 = gain_rows(2, f)

    def time_unpack(i):
        j = frame_id(i)
        arrived(t_in, t_sem, j)
        for fl in range(FL):
            row = lambda t: SPAN * t + 16 * (FL * j + fl)
            unpack_item(t_in, (j, fl), row, gk2, gv2)

    loop(NF, time_unpack)
    attend(q, ks, vs, g, kt, dq, dk, dv, s_scr, p_scr, SPAN, True)
    terms(1)
    share("space", s, NS, 1, at1, at1_sem)

    def time_back(i):
        j = frame_id(i)
        for fl in range(FL):
            row = lambda t: SPAN * t + 16 * (FL * j + fl)
            pack_item(tb_out, (j, fl), row, gk2, gv2)
        send("frame", f, j, tb_out, tb_in, send_sem.at[3], tb_sem)

    loop(NF, time_back)

    collect(f, NF, as1, as1_sem)
    a_out[2] = jnp.sum(as1[...], axis=0)
    share("space", s, NS, 2, as2, as2_sem)
    collect(s, NS, at1, at1_sem)
    a_out[3] = jnp.sum(at1[...], axis=0)
    share("frame", f, NF, 3, at2, at2_sem)

    def unpack_group(ref, leads, dst, fl, hg):
        heads = [unpack_tiles(*tiles_of(ref, lead)) for lead in leads]
        for t in range(4):
            pieces = join_heads(*(h[t] for h in heads))
            for c in range(3):
                cols = pl.ds(pl.multiple_of(hg * 384 + c * 128, 128), 128)
                dst[fl, pl.ds(16 * t, 16), cols] = pieces[c]

    def space_home(i):
        zi = space_z(i)
        for j in range(4):
            arrived(sb_in, sb_sem, 4 * zi + j)
        for n, dst in enumerate((dq_s, dk_s, dv_s)):
            unpack_group(sb_in, [(4 * zi + j, n) for j in range(4)], dst, zi // 4, zi % 4)

    loop(8, space_home)

    norm = float(SEQ * NF * FL) ** -0.5
    collect(s, NS, as2, as2_sem)
    collect(f, NF, at2, at2_sem)
    for hg in range(H // 4):
        for c, piece in enumerate(join_heads(*(as2[4 * hg + j] + as2[H + 4 * hg + j] for j in range(4)))):
            col = hg * 384 + c * 128
            ia3[0:2, col : col + 128] = piece[0:2] * norm
        for c, piece in enumerate(join_heads(*(at2[4 * hg + j] for j in range(4)))):
            col = hg * 384 + c * 128
            ia3[2:4, col : col + 128] = piece[0:2] * norm

    def time_home(hg):
        for j in range(4):
            arrived(tb_in, tb_sem, 4 * hg + j)
        for fl in range(FL):
            for n, dst in enumerate((dq_t, dk_t, dv_t)):
                unpack_group(tb_in, [(4 * hg + j, fl, n) for j in range(4)], dst, fl, hg)

    loop(H // 4, time_home)

    sent(s_out, NS, send_sem.at[0])
    sent(t_out, NF, send_sem.at[1])
    sent(sb_out, NS, send_sem.at[2])
    sent(tb_out, NF, send_sem.at[3])
    sent(as1, NF, a_send.at[0])
    sent(at1, NS, a_send.at[1])
    sent(as2, NS, a_send.at[2])
    sent(at2, NF, a_send.at[3])


def shards(*args):
    full = jax.ShapeDtypeStruct((FL, PL, H * HD), BF16)
    vmem = pl.BlockSpec(memory_space=pltpu.VMEM)
    operands = list(args[:7]) + [a.reshape(1, H * HD) for a in args[7:]]

    def nat(dtype):
        return pltpu.VMEM((SEQ, 128), dtype)

    dma = pltpu.SemaphoreType.DMA
    scratch = [
        pltpu.VMEM((NS, 4, ROWS, 128), BF16),
        pltpu.VMEM((NS, 4, ROWS, 128), BF16),
        pltpu.VMEM((NF, FL, 4, ROWS, 128), BF16),
        pltpu.VMEM((NF, FL, 4, ROWS, 128), BF16),
        pltpu.VMEM((NS, 3, ROWS, 128), BF16),
        pltpu.VMEM((NS, 3, ROWS, 128), BF16),
        pltpu.VMEM((NF, FL, 3, ROWS, 128), BF16),
        pltpu.VMEM((NF, FL, 3, ROWS, 128), BF16),
        *[nat(BF16) for _ in range(6)],
        pltpu.VMEM((128, SEQ), BF16),
        nat(BF16),
        nat(F32),
        nat(F32),
        pltpu.VMEM((SEQ, QB), F32),
        pltpu.VMEM((SEQ, QB), F32),
        pltpu.VMEM((4, H, 8, 128), F32),
        pltpu.VMEM((4, 8, 128), F32),
        pltpu.VMEM((NF, 8, 128), F32),
        pltpu.VMEM((NS, 8, 128), F32),
        pltpu.VMEM((NS, 8, 128), F32),
        pltpu.VMEM((NF, 8, 128), F32),
        dma((4,)),
        dma((NS,)),
        dma((NF,)),
        dma((NS,)),
        dma((NF,)),
        dma((4,)),
        dma((NF,)),
        dma((NS,)),
        dma((NS,)),
        dma((NF,)),
    ]
    return pl.pallas_call(
        kernel,
        out_shape=[full] * 6 + [jax.ShapeDtypeStruct((4, H * HD), F32)],
        in_specs=[vmem] * 11,
        out_specs=[vmem] * 7,
        scratch_shapes=scratch,
        compiler_params=pltpu.CompilerParams(
            collective_id=0, has_side_effects=True, vmem_limit_bytes=48 * 1024 * 1024
        ),
    )(*operands)


def solution(mesh):
    split = P("frame", "space", None)
    return jax.shard_map(
        shards,
        mesh=mesh,
        in_specs=(split,) * 7 + (P(),) * 4,
        out_specs=(split,) * 6 + (P(),),
        check_vma=False,
    )
```

```python
import functools

import jax
import jax.numpy as jnp
from jax import lax
from jax.experimental import pallas as pl
from jax.experimental.pallas import tpu as pltpu
from jax.sharding import PartitionSpec as P

F32, BF16 = jnp.float32, jnp.bfloat16
H = 16
HD = 96
NS = 32
NF = 16
FL = 2
PL = 64
SEQ = NS * PL
ROWS = PL * HD // 128
SPAN = 512
QB = 256
KT = 256
VMEM_LIMIT = 123 * 2**19
SCALE = HD**-0.5
LOG2E = 1.4426950408889634
NT = (((1,), (1,)), ((), ()))
NN = (((1,), (0,)), ((), ()))
MESH = pl.DeviceIdType.MESH


def mm(a, b, dims):
    return lax.dot_general(a, b, dims, preferred_element_type=F32)


def lanes(shape):
    return lax.broadcasted_iota(jnp.int32, shape, len(shape) - 1)


def split_heads(x):
    a, b, c = x[:, 0:128], x[:, 128:256], x[:, 256:384]
    lane = lanes(a.shape)
    return (
        a,
        jnp.where(lane < 32, pltpu.roll(a, 32, 1), pltpu.roll(b, 32, 1)),
        jnp.where(lane < 64, pltpu.roll(b, 64, 1), pltpu.roll(c, 64, 1)),
        pltpu.roll(c, 96, 1),
    )


def join_heads(w, x, y, z):
    lane = lanes(w.shape)
    x, y, z = pltpu.roll(x, 96, 1), pltpu.roll(y, 64, 1), pltpu.roll(z, 32, 1)
    return jnp.where(lane < 96, w, x), jnp.where(lane < 64, x, y), jnp.where(lane < 32, y, z)


def pack_tiles(t0, t1, t2, t3):
    lane = lanes(t0.shape)
    return (
        jnp.where(lane < 96, t0, pltpu.roll(t3, 96, 1)),
        jnp.where(lane < 96, t1, pltpu.roll(t3, 64, 1)),
        jnp.where(lane < 96, t2, pltpu.roll(t3, 32, 1)),
    )


def unpack_tiles(p0, p1, p2):
    lane = lanes(p0.shape)
    zero = jnp.zeros_like(p0)
    last = jnp.where(lane < 32, pltpu.roll(p0, 32, 1), pltpu.roll(p1, 64, 1))
    last = jnp.where(lane < 64, last, pltpu.roll(p2, 96, 1))
    return tuple(jnp.where(lane < 96, t, zero) for t in (p0, p1, p2, last))


def tiles_of(ref, lead, count=3):
    return [ref[(*lead, pl.ds(16 * t, 16), slice(None))] for t in range(count)]


def attend(q, ks, vs, g, kt, dq, dk, dv, s_scr, p_scr, span, masked):
    tiles = span // KT
    for c in range(SEQ // 128):
        kt[:, c * 128 : (c + 1) * 128] = ks[c * 128 : (c + 1) * 128, :].T
    dk[...] = jnp.zeros_like(dk)
    dv[...] = jnp.zeros_like(dv)

    def step(start, base):
        rows = pl.ds(pl.multiple_of(start, QB), QB)
        keys = [pl.ds(pl.multiple_of(base + t * KT, KT), KT) for t in range(tiles)]
        tile = [pl.ds(t * KT, KT) for t in range(tiles)]
        qi, gi = q[rows, :], g[rows, :]
        if masked:
            key_pos = lax.broadcasted_iota(jnp.int32, (KT, QB), 0) & 15
            same = key_pos == (lanes((KT, QB)) & 15)
        top = None
        for t in range(tiles):
            s = mm(ks[keys[t], :], qi, NT)
            if masked:
                s = jnp.where(same, s, -jnp.inf)
            s_scr[tile[t], :] = s
            here = jnp.max(s.reshape(KT // 8, 8, QB), axis=0)
            top = here if top is None else jnp.maximum(top, here)
        top = jnp.max(top, axis=0, keepdims=True)
        total = jnp.zeros((8, QB), F32)
        delta = jnp.zeros((8, QB), F32)
        for t in range(tiles):
            e = jnp.exp2((s_scr[tile[t], :] - top) * (SCALE * LOG2E))
            dp = mm(vs[keys[t], :], gi, NT)
            s_scr[tile[t], :] = e
            p_scr[tile[t], :] = dp
            total += jnp.sum(e.reshape(KT // 8, 8, QB), axis=0)
            delta += jnp.sum((e * dp).reshape(KT // 8, 8, QB), axis=0)
        inv = 1.0 / jnp.sum(total, axis=0, keepdims=True)
        delta = jnp.sum(delta, axis=0, keepdims=True) * inv
        dq_t = jnp.zeros((HD, QB), F32)
        for t in range(tiles):
            p = s_scr[tile[t], :] * inv
            ds = (p * (p_scr[tile[t], :] - delta) * SCALE).astype(BF16)
            dv[keys[t], :] += mm(p.astype(BF16), gi, NN)
            dk[keys[t], :] += mm(ds, qi, NN)
            dq_t += mm(kt[0:HD, keys[t]], ds, NN)
        dq[rows, 0:HD] = dq_t.T.astype(BF16)

    def outer(b, carry):
        for i in range(span // QB if masked else 1):
            step(b * (span if masked else QB) + i * QB, b * span if masked else 0)
        return carry

    lax.fori_loop(0, SEQ // (span if masked else QB), outer, 0)


def kernel(
    q_s_hbm, k_s_hbm, v_s_hbm, q_t_hbm, k_t_hbm, v_t_hbm, grad_hbm,
    gain_ks_hbm, gain_vs_hbm, gain_kt_hbm, gain_vt_hbm,
    dq_s_hbm, dk_s_hbm, dv_s_hbm, dq_t_hbm, dk_t_hbm, dv_t_hbm, ia3_hbm,
    q_s, k_s, v_s, q_t, k_t, v_t, grad, gain_ks, gain_vs, gain_kt, gain_vt, load_sem,
    dq_s, dk_s, dv_s, dq_t, dk_t, dv_t, ia3, store_sem,
    s_out, s_in, t_out, t_in, sb_out, sb_in, tb_out, tb_in,
    q, k, v, ks, vs, g, kt, dq, dk, dv, s_scr, p_scr, gains,
    a_out, as1, at1, as2, at2,
    send_sem, s_sem, t_sem, sb_sem, tb_sem, a_send, as1_sem, at1_sem, as2_sem, at2_sem,
):
    f = lax.axis_index("frame")
    s = lax.axis_index("space")
    z, y = s // 4, s % 4
    fx, fz, fc = f // 4, (f // 2) % 2, f % 2

    def space_id(i):
        zi, yi = i // 4, i % 4
        half = (z // 4 + 1 + zi // 4) % 2
        return (4 * half + (z + zi) % 4) * 4 + (y + yi) % 4

    def space_z(i):
        half = (z // 4 + 1 + i // 4) % 2
        return 4 * half + (z + i) % 4

    def frame_id(i):
        zi = (fz + 1 + i // 8) % 2
        return 4 * ((fx + i // 2) % 4) + 2 * zi + (fc + i) % 2

    def send(axis, me, to, src, dst, ssem, rsem):
        @pl.when(to != me)
        def _():
            pltpu.make_async_remote_copy(
                src.at[to], dst.at[me], ssem, rsem.at[me], device_id={axis: to}, device_id_type=MESH
            ).start()

        @pl.when(to == me)
        def _():
            pltpu.make_async_copy(src.at[me], dst.at[me], rsem.at[me]).start()

    def arrived(dst, rsem, j):
        pltpu.make_async_copy(dst.at[j], dst.at[j], rsem.at[j]).wait()

    def sent(src, n, sem):
        part = src.at[pl.ds(0, n - 1)]
        pltpu.make_async_copy(part, part, sem).wait()

    def loop(n, body):
        def run(i, carry):
            body(i)
            return carry

        lax.fori_loop(0, n, run, 0)

    names = ("grad", "q_s", "k_s", "v_s", "q_t", "k_t", "v_t")
    loads = {}
    for n, (name, src, dst) in enumerate(
        zip(
            names + ("gain_ks", "gain_vs", "gain_kt", "gain_vt"),
            (grad_hbm, q_s_hbm, k_s_hbm, v_s_hbm, q_t_hbm, k_t_hbm, v_t_hbm)
            + (gain_ks_hbm, gain_vs_hbm, gain_kt_hbm, gain_vt_hbm),
            (grad, q_s, k_s, v_s, q_t, k_t, v_t, gain_ks, gain_vs, gain_kt, gain_vt),
        )
    ):
        loads[name] = pltpu.make_async_copy(src, dst, load_sem.at[n])
        loads[name].start()

    barrier = pltpu.get_barrier_semaphore()

    def greet(axis, me, n):
        def body(i):
            pl.semaphore_signal(
                barrier, inc=1, device_id={axis: (me + 1 + i) % n}, device_id_type=MESH
            )

        loop(n - 1, body)

    greet("space", s, NS)
    greet("frame", f, NF)

    def pack_group(ref, fl, hg):
        cols = pl.ds(pl.multiple_of(hg * 384, 128), 384)
        heads = split_heads(ref[fl, :, cols])
        return [pack_tiles(*(x[16 * t : 16 * t + 16] for t in range(4))) for x in heads]

    def put(ref, lead, tiles):
        for t in range(3):
            ref[(*lead, pl.ds(16 * t, 16), slice(None))] = tiles[t]

    for name in names[:4]:
        loads[name].wait()
    pl.semaphore_wait(barrier, NS + NF - 2)

    def space_pack(i):
        zi = space_z(i)
        fl, hg = zi // 4, zi % 4
        for n, ref in enumerate((q_s, k_s, v_s, grad)):
            packed = pack_group(ref, fl, hg)
            for j in range(4):
                put(s_out, (4 * zi + j, n), packed[j])
        for j in range(4):
            send("space", s, 4 * zi + (y + j) % 4, s_out, s_in, send_sem.at[0], s_sem)

    loop(8, space_pack)

    for name in names[4:]:
        loads[name].wait()

    def frame_send(to):
        send("frame", f, to, t_out, t_in, send_sem.at[1], t_sem)

    def time_pack(i):
        hg = (fx + i) % 4
        for fl in range(FL):
            for n, ref in enumerate((q_t, k_t, v_t, grad)):
                packed = pack_group(ref, fl, hg)
                for j in range(4):
                    put(t_out, (4 * hg + j, fl, n), packed[j])
        for j in range(2):
            frame_send(4 * hg + 2 * (1 - fz) + (fc + j) % 2)

    loop(4, time_pack)
    loop(8, lambda i: frame_send(frame_id(8 + i)))

    for name in ("gain_ks", "gain_vs", "gain_kt", "gain_vt"):
        loads[name].wait()

    for i in range(H // 4):
        for r, ref in enumerate((gain_ks, gain_vs, gain_kt, gain_vt)):
            heads = split_heads(jnp.broadcast_to(ref[384 * i : 384 * i + 384].reshape(1, 384), (8, 384)))
            for j in range(4):
                gains[r, 4 * i + j] = heads[j]


    def unpack_item(ref, lead, row_of, gain_k, gain_v):
        for n, dst in enumerate((q, k, v, g)):
            tiles = unpack_tiles(*tiles_of(ref, (*lead, n)))
            for t in range(4):
                rows = pl.ds(pl.multiple_of(row_of(t), 16), 16)
                dst[rows, :] = tiles[t]
                if n == 1:
                    ks[rows, :] = (tiles[t].astype(F32) * gain_k).astype(BF16)
                if n == 2:
                    vs[rows, :] = (tiles[t].astype(F32) * gain_v).astype(BF16)

    def pack_item(ref, lead, row_of, gain_k, gain_v):
        for n, src in enumerate((dq, dk, dv)):
            tiles = []
            for t in range(4):
                x = src[pl.ds(pl.multiple_of(row_of(t), 16), 16), :]
                if n:
                    gain = gain_k if n == 1 else gain_v
                    x = (x.astype(BF16).astype(F32) * gain).astype(BF16)
                tiles.append(x)
            put(ref, (*lead, n), pack_tiles(*tiles))

    def gain_rows(row, head):
        return gains[row, head, 0:1, :], gains[row + 1, head, 0:1, :]

    def terms(slot):
        def body(i, carry):
            rows = pl.ds(pl.multiple_of(i * 128, 128), 128)
            out = []
            for acc, a, b in ((carry[0], dk, k), (carry[1], dv, v)):
                prod = a[rows, :].astype(BF16).astype(F32) * b[rows, :].astype(F32)
                out.append(acc + jnp.sum(prod.reshape(16, 8, 128), axis=0))
            return tuple(out)

        zero = jnp.zeros((8, 128), F32)
        tk, tv = lax.fori_loop(0, SEQ // 128, body, (zero, zero))
        a_out[slot] = jnp.concatenate(
            [jnp.sum(tk, axis=0, keepdims=True), jnp.sum(tv, axis=0, keepdims=True)]
        )

    def share(axis, me, n, slot, dst, rsem):
        dst[me] = a_out[slot]

        def body(i):
            pltpu.make_async_remote_copy(
                a_out.at[slot],
                dst.at[me],
                a_send.at[slot],
                rsem.at[me],
                device_id={axis: (me + 1 + i) % n},
                device_id_type=MESH,
            ).start()

        loop(n - 1, body)

    def collect(me, n, dst, rsem):
        loop(n - 1, lambda i: arrived(dst, rsem, (me + 1 + i) % n))

    dq[...] = jnp.zeros_like(dq)

    gk_s, gv_s = gain_rows(0, s % H)

    def space_unpack(i):
        j = space_id(i)
        arrived(s_in, s_sem, j)
        unpack_item(s_in, (j,), lambda t: PL * j + 16 * t, gk_s, gv_s)

    loop(NS, space_unpack)
    attend(q, ks, vs, g, kt, dq, dk, dv, s_scr, p_scr, SEQ, False)
    terms(0)
    share("frame", f, NF, 0, as1, as1_sem)

    def space_back(i):
        j = space_id(i)
        pack_item(sb_out, (j,), lambda t: PL * j + 16 * t, gk_s, gv_s)
        send("space", s, j, sb_out, sb_in, send_sem.at[2], sb_sem)

    loop(NS, space_back)

    gk_t, gv_t = gain_rows(2, f)

    def time_row(j, fl):
        return lambda t: SPAN * t + 16 * (FL * j + fl)

    def time_unpack(i):
        j = frame_id(i)
        arrived(t_in, t_sem, j)
        for fl in range(FL):
            unpack_item(t_in, (j, fl), time_row(j, fl), gk_t, gv_t)

    loop(NF, time_unpack)
    collect(f, NF, as1, as1_sem)
    a_out[2] = jnp.sum(as1[...], axis=0)
    share("space", s, NS, 2, as2, as2_sem)
    attend(q, ks, vs, g, kt, dq, dk, dv, s_scr, p_scr, SPAN, True)
    terms(1)
    share("space", s, NS, 1, at1, at1_sem)

    def time_back(i):
        j = frame_id(i)
        for fl in range(FL):
            pack_item(tb_out, (j, fl), time_row(j, fl), gk_t, gv_t)
        send("frame", f, j, tb_out, tb_in, send_sem.at[3], tb_sem)

    loop(NF // 4, time_back)

    def unpack_group(ref, leads, dst, fl, hg):
        heads = [unpack_tiles(*tiles_of(ref, lead)) for lead in leads]
        for t in range(4):
            pieces = join_heads(*(h[t] for h in heads))
            for c in range(3):
                cols = pl.ds(pl.multiple_of(hg * 384 + c * 128, 128), 128)
                dst[fl, pl.ds(16 * t, 16), cols] = pieces[c]

    stores = []

    def store(src, dst):
        copy = pltpu.make_async_copy(src, dst, store_sem.at[len(stores)])
        copy.start()
        stores.append(copy)

    def space_home(i):
        zi = space_z(i)
        for j in range(4):
            arrived(sb_in, sb_sem, 4 * zi + j)
        for n, dst in enumerate((dq_s, dk_s, dv_s)):
            unpack_group(sb_in, [(4 * zi + j, n) for j in range(4)], dst, zi // 4, zi % 4)

    loop(8, space_home)
    for src, dst in ((dq_s, dq_s_hbm), (dk_s, dk_s_hbm), (dv_s, dv_s_hbm)):
        store(src, dst)
    collect(s, NS, at1, at1_sem)
    a_out[3] = jnp.sum(at1[...], axis=0)
    share("frame", f, NF, 3, at2, at2_sem)
    loop(NF - NF // 4, lambda i: time_back(NF // 4 + i))
    collect(s, NS, as2, as2_sem)

    def time_home(hg):
        for j in range(4):
            arrived(tb_in, tb_sem, 4 * hg + j)
        for fl in range(FL):
            for n, dst in enumerate((dq_t, dk_t, dv_t)):
                unpack_group(tb_in, [(4 * hg + j, fl, n) for j in range(4)], dst, fl, hg)

    loop(H // 4, time_home)
    for src, dst in ((dq_t, dq_t_hbm), (dk_t, dk_t_hbm), (dv_t, dv_t_hbm)):
        store(src, dst)

    norm = float(SEQ * NF * FL) ** -0.5
    collect(f, NF, at2, at2_sem)
    for hg in range(H // 4):
        space = [as2[4 * hg + j] + as2[H + 4 * hg + j] for j in range(4)]
        time = [at2[4 * hg + j] for j in range(4)]
        for row, heads in ((0, space), (2, time)):
            for c, piece in enumerate(join_heads(*heads)):
                col = hg * 384 + c * 128
                ia3[row : row + 2, col : col + 128] = piece * norm
    store(ia3, ia3_hbm)

    sent(s_out, NS, send_sem.at[0])
    sent(t_out, NF, send_sem.at[1])
    sent(sb_out, NS, send_sem.at[2])
    sent(tb_out, NF, send_sem.at[3])
    sent(as1, NF, a_send.at[0])
    sent(at1, NS, a_send.at[1])
    sent(as2, NS, a_send.at[2])
    sent(at2, NF, a_send.at[3])
    for copy in stores:
        copy.wait()


def write_out(*refs):
    n = len(refs) // 3
    sems = refs[-1]
    loads = [pltpu.make_async_copy(refs[i], refs[2 * n + i], sems.at[i]) for i in range(n)]
    stores = [pltpu.make_async_copy(refs[2 * n + i], refs[n + i], sems.at[n + i]) for i in range(n)]
    for load in loads:
        load.start()
    for load, store in zip(loads, stores):
        load.wait()
        store.start()
    for store in stores:
        store.wait()


def shards(*args):
    full = jax.ShapeDtypeStruct((FL, PL, H * HD), BF16)
    hbm = pl.BlockSpec(memory_space=pltpu.HBM)

    def nat(dtype):
        return pltpu.VMEM((SEQ, 128), dtype)

    dma = pltpu.SemaphoreType.DMA
    scratch = [
        *[pltpu.VMEM((FL, PL, H * HD), BF16) for _ in range(7)],
        *[pltpu.VMEM((H * HD,), F32) for _ in range(4)],
        dma((11,)),
        *[pltpu.VMEM((FL, PL, H * HD), BF16) for _ in range(6)],
        pltpu.VMEM((4, H * HD), F32),
        dma((7,)),
        pltpu.VMEM((NS, 4, ROWS, 128), BF16),
        pltpu.VMEM((NS, 4, ROWS, 128), BF16),
        pltpu.VMEM((NF, FL, 4, ROWS, 128), BF16),
        pltpu.VMEM((NF, FL, 4, ROWS, 128), BF16),
        pltpu.VMEM((NS, 3, ROWS, 128), BF16),
        pltpu.VMEM((NS, 3, ROWS, 128), BF16),
        pltpu.VMEM((NF, FL, 3, ROWS, 128), BF16),
        pltpu.VMEM((NF, FL, 3, ROWS, 128), BF16),
        *[nat(BF16) for _ in range(6)],
        pltpu.VMEM((128, SEQ), BF16),
        nat(BF16),
        nat(F32),
        nat(F32),
        pltpu.VMEM((SEQ, QB), F32),
        pltpu.VMEM((SEQ, QB), F32),
        pltpu.VMEM((4, H, 8, 128), F32),
        *[pltpu.VMEM((n, 2, 128), F32) for n in (4, NF, NS, NS, NF)],
        dma((4,)),
        dma((NS,)),
        dma((NF,)),
        dma((NS,)),
        dma((NF,)),
        dma((4,)),
        dma((NF,)),
        dma((NS,)),
        dma((NS,)),
        dma((NF,)),
    ]
    out_shape = [full] * 6 + [jax.ShapeDtypeStruct((4, H * HD), F32)]
    results = pl.pallas_call(
        kernel,
        out_shape=out_shape,
        in_specs=[hbm] * 11,
        out_specs=[hbm] * 7,
        scratch_shapes=scratch,
        compiler_params=pltpu.CompilerParams(
            collective_id=0, has_side_effects=True, vmem_limit_bytes=VMEM_LIMIT
        ),
    )(*args)
    return pl.pallas_call(
        write_out,
        out_shape=out_shape,
        in_specs=[hbm] * 7,
        out_specs=[hbm] * 7,
        scratch_shapes=[pltpu.VMEM(a.shape, a.dtype) for a in out_shape] + [dma((14,))],
        compiler_params=pltpu.CompilerParams(vmem_limit_bytes=VMEM_LIMIT),
    )(*results)


def solution(mesh):
    split = P("frame", "space", None)
    return jax.shard_map(
        shards,
        mesh=mesh,
        in_specs=(split,) * 7 + (P(),) * 4,
        out_specs=(split,) * 6 + (P(),),
        check_vma=False,
    )
```

```python
import functools

import functools

import jax
import jax.numpy as jnp
from jax import lax
from jax.experimental import pallas as pl
from jax.experimental.pallas import tpu as pltpu
from jax.sharding import PartitionSpec as P

F32, BF16 = jnp.float32, jnp.bfloat16
H = 16
HD = 96
NS = 32
NF = 16
FL = 2
PL = 64
SEQ = NS * PL
ROWS = PL * HD // 128
SPAN = 512
QB = 256
KT = 256
VMEM_LIMIT = 123 * 2**19
SCALE = HD**-0.5
LOG2E = 1.4426950408889634
NT = (((1,), (1,)), ((), ()))
NN = (((1,), (0,)), ((), ()))
MESH = pl.DeviceIdType.MESH


def mm(a, b, dims):
    return lax.dot_general(a, b, dims, preferred_element_type=F32)


def lanes(shape):
    return lax.broadcasted_iota(jnp.int32, shape, len(shape) - 1)


def split_heads(x):
    a, b, c = x[:, 0:128], x[:, 128:256], x[:, 256:384]
    lane = lanes(a.shape)
    return (
        a,
        jnp.where(lane < 32, pltpu.roll(a, 32, 1), pltpu.roll(b, 32, 1)),
        jnp.where(lane < 64, pltpu.roll(b, 64, 1), pltpu.roll(c, 64, 1)),
        pltpu.roll(c, 96, 1),
    )


def join_heads(w, x, y, z):
    lane = lanes(w.shape)
    x, y, z = pltpu.roll(x, 96, 1), pltpu.roll(y, 64, 1), pltpu.roll(z, 32, 1)
    return jnp.where(lane < 96, w, x), jnp.where(lane < 64, x, y), jnp.where(lane < 32, y, z)


def pack_tiles(t0, t1, t2, t3):
    lane = lanes(t0.shape)
    return (
        jnp.where(lane < 96, t0, pltpu.roll(t3, 96, 1)),
        jnp.where(lane < 96, t1, pltpu.roll(t3, 64, 1)),
        jnp.where(lane < 96, t2, pltpu.roll(t3, 32, 1)),
    )


def unpack_tiles(p0, p1, p2):
    lane = lanes(p0.shape)
    zero = jnp.zeros_like(p0)
    last = jnp.where(lane < 32, pltpu.roll(p0, 32, 1), pltpu.roll(p1, 64, 1))
    last = jnp.where(lane < 64, last, pltpu.roll(p2, 96, 1))
    return tuple(jnp.where(lane < 96, t, zero) for t in (p0, p1, p2, last))


def tiles_of(ref, lead, count=3):
    return [ref[(*lead, pl.ds(16 * t, 16), slice(None))] for t in range(count)]


def attend(q, ks, vs, g, kt, dq, dk, dv, s_scr, p_scr, span, masked):
    tiles = span // KT
    for c in range(SEQ // 128):
        kt[:, c * 128 : (c + 1) * 128] = ks[c * 128 : (c + 1) * 128, :].T
    dk[...] = jnp.zeros_like(dk)
    dv[...] = jnp.zeros_like(dv)

    def step(start, base):
        rows = pl.ds(pl.multiple_of(start, QB), QB)
        keys = [pl.ds(pl.multiple_of(base + t * KT, KT), KT) for t in range(tiles)]
        tile = [pl.ds(t * KT, KT) for t in range(tiles)]
        qi, gi = q[rows, :], g[rows, :]
        if masked:
            key_pos = lax.broadcasted_iota(jnp.int32, (KT, QB), 0) & 15
            same = key_pos == (lanes((KT, QB)) & 15)
        top = None
        for t in range(tiles):
            s = mm(ks[keys[t], :], qi, NT)
            if masked:
                s = jnp.where(same, s, -jnp.inf)
            s_scr[tile[t], :] = s
            here = jnp.max(s.reshape(KT // 8, 8, QB), axis=0)
            top = here if top is None else jnp.maximum(top, here)
        top = jnp.max(top, axis=0, keepdims=True)
        total = jnp.zeros((8, QB), F32)
        delta = jnp.zeros((8, QB), F32)
        for t in range(tiles):
            e = jnp.exp2((s_scr[tile[t], :] - top) * (SCALE * LOG2E))
            dp = mm(vs[keys[t], :], gi, NT)
            s_scr[tile[t], :] = e
            p_scr[tile[t], :] = dp
            total += jnp.sum(e.reshape(KT // 8, 8, QB), axis=0)
            delta += jnp.sum((e * dp).reshape(KT // 8, 8, QB), axis=0)
        inv = 1.0 / jnp.sum(total, axis=0, keepdims=True)
        delta = jnp.sum(delta, axis=0, keepdims=True) * inv
        dq_t = jnp.zeros((HD, QB), F32)
        for t in range(tiles):
            p = s_scr[tile[t], :] * inv
            ds = (p * (p_scr[tile[t], :] - delta) * SCALE).astype(BF16)
            dv[keys[t], :] += mm(p.astype(BF16), gi, NN)
            dk[keys[t], :] += mm(ds, qi, NN)
            dq_t += mm(kt[0:HD, keys[t]], ds, NN)
        dq[rows, 0:HD] = dq_t.T.astype(BF16)

    def outer(b, carry):
        for i in range(span // QB if masked else 1):
            step(b * (span if masked else QB) + i * QB, b * span if masked else 0)
        return carry

    lax.fori_loop(0, SEQ // (span if masked else QB), outer, 0)


def kernel(
    q_s_hbm, k_s_hbm, v_s_hbm, q_t_hbm, k_t_hbm, v_t_hbm, grad_hbm,
    gain_ks_hbm, gain_vs_hbm, gain_kt_hbm, gain_vt_hbm,
    dq_s_hbm, dk_s_hbm, dv_s_hbm, dq_t_hbm, dk_t_hbm, dv_t_hbm, ia3_hbm,
    q_s, k_s, v_s, q_t, k_t, v_t, grad, gain_ks, gain_vs, gain_kt, gain_vt, load_sem,
    dq_s, dk_s, dv_s, dq_t, dk_t, dv_t, ia3, store_sem,
    s_out, s_in, t_out, t_in, tg_out, tg_in, sb_out, sb_in, tb_out, tb_in,
    q, k, v, ks, vs, g, kt, dq, dk, dv, s_scr, p_scr, gains,
    a_out, a_out2, as1, at1, as2, at2,
    tg_sem, send_sem, s_sem, t_sem, sb_sem, tb_sem, a_send, as1_sem, at1_sem, as2_sem, at2_sem,
):
    f = lax.axis_index("frame")
    s = lax.axis_index("space")
    z, y = s // 4, s % 4
    fx, fz, fc = f // 4, (f // 2) % 2, f % 2
    half = s // 16
    s_set, s_fl, s_place = (half + fz) % 2, (s // 8) % 2, s % 8
    t_set, t_place = (fz + half) % 2, 2 * fx + fc

    def group_of_z(zi):
        return (zi // 2) % 2, 2 * ((zi // 4 + fz) % 2) + zi % 2

    def frame_of(hg, j):
        return 4 * (2 * (hg % 2) + j // 2) + 2 * ((hg // 2 + half) % 2) + j % 2

    def space_id(i):
        zi, yi = i // 4, i % 4
        zi_half = (z // 4 + 1 + zi // 4) % 2
        return (4 * zi_half + (z + zi) % 4) * 4 + (y + yi) % 4

    def space_z(i):
        zi_half = (z // 4 + 1 + i // 4) % 2
        return 4 * zi_half + (z + i) % 4

    def frame_id(i):
        zi = (fz + 1 + i // 8) % 2
        return 4 * ((fx + i // 2) % 4) + 2 * zi + (fc + i) % 2

    def send(axis, me, to, src, dst, ssem, rsem):
        @pl.when(to != me)
        def _():
            pltpu.make_async_remote_copy(
                src.at[to], dst.at[me], ssem, rsem.at[me], device_id={axis: to}, device_id_type=MESH
            ).start()

        @pl.when(to == me)
        def _():
            pltpu.make_async_copy(src.at[me], dst.at[me], rsem.at[me]).start()

    def arrived(dst, rsem, j):
        pltpu.make_async_copy(dst.at[j], dst.at[j], rsem.at[j]).wait()

    def sent(src, n, sem):
        part = src.at[pl.ds(0, n - 1)]
        pltpu.make_async_copy(part, part, sem).wait()

    def loop(n, body):
        def run(i, carry):
            body(i)
            return carry

        lax.fori_loop(0, n, run, 0)

    names = ("grad", "q_s", "k_s", "v_s", "q_t", "k_t", "v_t")
    loads = {}
    for n, (name, src, dst) in enumerate(
        zip(
            names + ("gain_ks", "gain_vs", "gain_kt", "gain_vt"),
            (grad_hbm, q_s_hbm, k_s_hbm, v_s_hbm, q_t_hbm, k_t_hbm, v_t_hbm)
            + (gain_ks_hbm, gain_vs_hbm, gain_kt_hbm, gain_vt_hbm),
            (grad, q_s, k_s, v_s, q_t, k_t, v_t, gain_ks, gain_vs, gain_kt, gain_vt),
        )
    ):
        loads[name] = pltpu.make_async_copy(src, dst, load_sem.at[n])
        loads[name].start()

    barrier = pltpu.get_barrier_semaphore()

    def greet(axis, me, n):
        def body(i):
            pl.semaphore_signal(
                barrier, inc=1, device_id={axis: (me + 1 + i) % n}, device_id_type=MESH
            )

        loop(n - 1, body)

    greet("space", s, NS)
    greet("frame", f, NF)

    def greet_items(i):
        at = {"frame": 4 * (i // 4) + 2 * (1 - fz) + (i // 2) % 2}
        at["space"] = 16 * (1 - half) + 8 * (i % 2) + t_place
        pl.semaphore_signal(barrier, inc=1, device_id=at, device_id_type=MESH)

    loop(16, greet_items)

    def pack_group(ref, fl, hg):
        cols = pl.ds(pl.multiple_of(hg * 384, 128), 384)
        heads = split_heads(ref[fl, :, cols])
        return [pack_tiles(*(x[16 * t : 16 * t + 16] for t in range(4))) for x in heads]

    def put(ref, lead, tiles):
        for t in range(3):
            ref[(*lead, pl.ds(16 * t, 16), slice(None))] = tiles[t]

    for name in names[:4]:
        loads[name].wait()
    pl.semaphore_wait(barrier, NS + NF - 2 + 16)

    def space_pack(i):
        zi = space_z(i)
        fl, hg = group_of_z(zi)
        for n, ref in enumerate((q_s, k_s, v_s, grad)):
            packed = pack_group(ref, fl, hg)
            for j in range(4):
                put(s_out, (4 * zi + j, n), packed[j])
        for j in range(4):
            send("space", s, 4 * zi + (y + j) % 4, s_out, s_in, send_sem.at[0], s_sem)

    loop(8, space_pack)

    for name in names[4:]:
        loads[name].wait()

    def time_pack(hg):
        for fl in range(FL):
            for n, ref in enumerate((q_t, k_t, v_t, grad)):
                packed = pack_group(ref, fl, hg)
                for j in range(4):
                    if n == 3:
                        put(tg_out, (frame_of(hg, j), fl), packed[j])
                    else:
                        put(t_out, (frame_of(hg, j), fl, n), packed[j])

    loop(4, time_pack)

    def time_send(i):
        send("frame", f, frame_id(i), t_out, t_in, send_sem.at[1], t_sem)

    def time_send_near(i):
        time_send(8 + i)
        send("frame", f, frame_id(8 + i), tg_out, tg_in, send_sem.at[4], tg_sem)

    loop(8, time_send)
    loop(8, time_send_near)

    for name in ("gain_ks", "gain_vs", "gain_kt", "gain_vt"):
        loads[name].wait()

    for i in range(H // 4):
        for r, ref in enumerate((gain_ks, gain_vs, gain_kt, gain_vt)):
            heads = split_heads(jnp.broadcast_to(ref[384 * i : 384 * i + 384].reshape(1, 384), (8, 384)))
            for j in range(4):
                gains[r, 4 * i + j] = heads[j]


    def unpack_item(leads, row_of, gain_k, gain_v):
        for n, dst in enumerate((q, k, v, g)):
            tiles = unpack_tiles(*tiles_of(*leads[n]))
            for t in range(4):
                rows = pl.ds(pl.multiple_of(row_of(t), 16), 16)
                dst[rows, :] = tiles[t]
                if n == 1:
                    ks[rows, :] = (tiles[t].astype(F32) * gain_k).astype(BF16)
                if n == 2:
                    vs[rows, :] = (tiles[t].astype(F32) * gain_v).astype(BF16)

    def pack_item(ref, lead, row_of, gain_k, gain_v):
        for n, src in enumerate((dq, dk, dv)):
            tiles = []
            for t in range(4):
                x = src[pl.ds(pl.multiple_of(row_of(t), 16), 16), :]
                if n:
                    gain = gain_k if n == 1 else gain_v
                    x = (x.astype(BF16).astype(F32) * gain).astype(BF16)
                tiles.append(x)
            put(ref, (*lead, n), pack_tiles(*tiles))

    def gain_rows(row, head):
        return gains[row, head, 0:1, :], gains[row + 1, head, 0:1, :]

    def terms(slot):
        def body(i, carry):
            rows = pl.ds(pl.multiple_of(i * 128, 128), 128)
            out = []
            for acc, a, b in ((carry[0], dk, k), (carry[1], dv, v)):
                prod = a[rows, :].astype(BF16).astype(F32) * b[rows, :].astype(F32)
                out.append(acc + jnp.sum(prod.reshape(16, 8, 128), axis=0))
            return tuple(out)

        zero = jnp.zeros((8, 128), F32)
        tk, tv = lax.fori_loop(0, SEQ // 128, body, (zero, zero))
        a_out[slot] = jnp.concatenate(
            [jnp.sum(tk, axis=0, keepdims=True), jnp.sum(tv, axis=0, keepdims=True)]
        )

    def share(axis, me, n, block, slot, dst, rsem):
        dst[me] = block[...]

        def body(i):
            pltpu.make_async_remote_copy(
                block,
                dst.at[me],
                a_send.at[slot],
                rsem.at[me],
                device_id={axis: (me + 1 + i) % n},
                device_id_type=MESH,
            ).start()

        loop(n - 1, body)

    def collect(me, n, dst, rsem):
        loop(n - 1, lambda i: arrived(dst, rsem, (me + 1 + i) % n))

    dq[...] = jnp.zeros_like(dq)

    gk_s, gv_s = gain_rows(0, 8 * s_set + s_place)

    def space_unpack(i):
        j = space_id(i)
        arrived(s_in, s_sem, j)
        unpack_item([(s_in, (j, n)) for n in range(4)], lambda t: PL * j + 16 * t, gk_s, gv_s)

    def space_unpack_far(i):
        space_unpack(i)
        j = space_id(i)
        at = {"frame": 4 * (s_place // 2) + 2 * (1 - fz) + s_place % 2, "space": j}
        pltpu.make_async_remote_copy(
            s_in.at[j, 3],
            tg_in.at[f, s_fl],
            send_sem.at[5],
            tg_sem.at[f],
            device_id=at,
            device_id_type=MESH,
        ).start()

    loop(NS // 2, space_unpack_far)
    loop(NS // 2, lambda i: space_unpack(NS // 2 + i))
    attend(q, ks, vs, g, kt, dq, dk, dv, s_scr, p_scr, SEQ, False)
    terms(0)
    share("frame", f, NF, a_out.at[0], 0, as1, as1_sem)

    def space_back(i):
        j = space_id(i)
        pack_item(sb_out, (j,), lambda t: PL * j + 16 * t, gk_s, gv_s)
        send("space", s, j, sb_out, sb_in, send_sem.at[2], sb_sem)

    loop(NS, space_back)

    gk_t, gv_t = gain_rows(2, 8 * t_set + t_place)

    def time_row(j, fl):
        return lambda t: SPAN * t + 16 * (FL * j + fl)

    def time_unpack(i):
        j = frame_id(i)
        arrived(t_in, t_sem, j)
        arrived(tg_in, tg_sem, j)
        for fl in range(FL):
            leads = [(t_in, (j, fl, n)) for n in range(3)] + [(tg_in, (j, fl))]
            unpack_item(leads, time_row(j, fl), gk_t, gv_t)

    loop(NF, time_unpack)
    collect(f, NF, as1, as1_sem)
    for r in range(2):
        parts = [as1[4 * x + 2 * r + c] for x in range(4) for c in range(2)]
        a_out2[0, 2 * r : 2 * r + 2, :] = functools.reduce(jnp.add, parts)
    share("space", s, NS, a_out2.at[0], 2, as2, as2_sem)
    attend(q, ks, vs, g, kt, dq, dk, dv, s_scr, p_scr, SPAN, True)
    terms(1)
    share("space", s, NS, a_out.at[1], 1, at1, at1_sem)

    def time_back(i):
        j = frame_id(i)
        for fl in range(FL):
            pack_item(tb_out, (j, fl), time_row(j, fl), gk_t, gv_t)
        send("frame", f, j, tb_out, tb_in, send_sem.at[3], tb_sem)

    loop(NF // 4, time_back)

    def unpack_group(ref, leads, dst, fl, hg):
        heads = [unpack_tiles(*tiles_of(ref, lead)) for lead in leads]
        for t in range(4):
            pieces = join_heads(*(h[t] for h in heads))
            for c in range(3):
                cols = pl.ds(pl.multiple_of(hg * 384 + c * 128, 128), 128)
                dst[fl, pl.ds(16 * t, 16), cols] = pieces[c]

    stores = []

    def store(src, dst):
        copy = pltpu.make_async_copy(src, dst, store_sem.at[len(stores)])
        copy.start()
        stores.append(copy)

    def space_home(i):
        zi = space_z(i)
        for j in range(4):
            arrived(sb_in, sb_sem, 4 * zi + j)
        fl, hg = group_of_z(zi)
        for n, dst in enumerate((dq_s, dk_s, dv_s)):
            unpack_group(sb_in, [(4 * zi + j, n) for j in range(4)], dst, fl, hg)

    loop(8, space_home)
    for src, dst in ((dq_s, dq_s_hbm), (dk_s, dk_s_hbm), (dv_s, dv_s_hbm)):
        store(src, dst)
    collect(s, NS, at1, at1_sem)
    for b in range(2):
        a_out2[1, 2 * b : 2 * b + 2, :] = jnp.sum(at1[16 * b : 16 * b + 16], axis=0)
    share("frame", f, NF, a_out2.at[1], 3, at2, at2_sem)
    loop(NF - NF // 4, lambda i: time_back(NF // 4 + i))
    collect(s, NS, as2, as2_sem)

    def time_home(hg):
        for j in range(4):
            arrived(tb_in, tb_sem, frame_of(hg, j))
        for fl in range(FL):
            for n, dst in enumerate((dq_t, dk_t, dv_t)):
                unpack_group(tb_in, [(frame_of(hg, j), fl, n) for j in range(4)], dst, fl, hg)

    loop(H // 4, time_home)
    for src, dst in ((dq_t, dq_t_hbm), (dk_t, dk_t_hbm), (dv_t, dv_t_hbm)):
        store(src, dst)

    norm = float(SEQ * NF * FL) ** -0.5
    collect(f, NF, at2, at2_sem)
    for hg in range(H // 4):
        e, space, time = hg // 2, [], []
        for j in range(4):
            place = 4 * (hg % 2) + j
            here, there = 16 * e + place, 16 * (1 - e) + place
            space.append(
                (as2[here, 0:2, :] + as2[here + 8, 0:2, :])
                + (as2[there, 2:4, :] + as2[there + 8, 2:4, :])
            )
            peer = 4 * (place // 2) + place % 2
            time.append(at2[peer + 2 * e, 0:2, :] + at2[peer + 2 * (1 - e), 2:4, :])
        for row, heads in ((0, space), (2, time)):
            for c, piece in enumerate(join_heads(*heads)):
                col = hg * 384 + c * 128
                ia3[row : row + 2, col : col + 128] = piece * norm
    store(ia3, ia3_hbm)

    sent(s_out, NS, send_sem.at[0])
    sent(t_out, NF, send_sem.at[1])
    sent(tg_out, 8, send_sem.at[4])
    sent(tg_in, 9, send_sem.at[5])
    sent(sb_out, NS, send_sem.at[2])
    sent(tb_out, NF, send_sem.at[3])
    sent(as1, NF, a_send.at[0])
    sent(at1, NS, a_send.at[1])
    sent(as2, NS, a_send.at[2])
    sent(at2, NF, a_send.at[3])
    for copy in stores:
        copy.wait()


def write_out(*refs):
    n = len(refs) // 3
    sems = refs[-1]
    loads = [pltpu.make_async_copy(refs[i], refs[2 * n + i], sems.at[i]) for i in range(n)]
    stores = [pltpu.make_async_copy(refs[2 * n + i], refs[n + i], sems.at[n + i]) for i in range(n)]
    for load in loads:
        load.start()
    for load, store in zip(loads, stores):
        load.wait()
        store.start()
    for store in stores:
        store.wait()


def shards(*args):
    full = jax.ShapeDtypeStruct((FL, PL, H * HD), BF16)
    hbm = pl.BlockSpec(memory_space=pltpu.HBM)

    def nat(dtype):
        return pltpu.VMEM((SEQ, 128), dtype)

    dma = pltpu.SemaphoreType.DMA
    scratch = [
        *[pltpu.VMEM((FL, PL, H * HD), BF16) for _ in range(7)],
        *[pltpu.VMEM((H * HD,), F32) for _ in range(4)],
        dma((11,)),
        *[pltpu.VMEM((FL, PL, H * HD), BF16) for _ in range(6)],
        pltpu.VMEM((4, H * HD), F32),
        dma((7,)),
        pltpu.VMEM((NS, 4, ROWS, 128), BF16),
        pltpu.VMEM((NS, 4, ROWS, 128), BF16),
        pltpu.VMEM((NF, FL, 3, ROWS, 128), BF16),
        pltpu.VMEM((NF, FL, 3, ROWS, 128), BF16),
        pltpu.VMEM((NF, FL, ROWS, 128), BF16),
        pltpu.VMEM((NF, FL, ROWS, 128), BF16),
        pltpu.VMEM((NS, 3, ROWS, 128), BF16),
        pltpu.VMEM((NS, 3, ROWS, 128), BF16),
        pltpu.VMEM((NF, FL, 3, ROWS, 128), BF16),
        pltpu.VMEM((NF, FL, 3, ROWS, 128), BF16),
        *[nat(BF16) for _ in range(6)],
        pltpu.VMEM((128, SEQ), BF16),
        nat(BF16),
        nat(F32),
        nat(F32),
        pltpu.VMEM((SEQ, QB), F32),
        pltpu.VMEM((SEQ, QB), F32),
        pltpu.VMEM((4, H, 8, 128), F32),
        *[pltpu.VMEM((n, r, 128), F32) for n, r in ((2, 2), (2, 4), (NF, 2), (NS, 2), (NS, 4), (NF, 4))],
        dma((NF,)),
        dma((6,)),
        dma((NS,)),
        dma((NF,)),
        dma((NS,)),
        dma((NF,)),
        dma((4,)),
        dma((NF,)),
        dma((NS,)),
        dma((NS,)),
        dma((NF,)),
    ]
    out_shape = [full] * 6 + [jax.ShapeDtypeStruct((4, H * HD), F32)]
    results = pl.pallas_call(
        kernel,
        out_shape=out_shape,
        in_specs=[hbm] * 11,
        out_specs=[hbm] * 7,
        scratch_shapes=scratch,
        compiler_params=pltpu.CompilerParams(
            collective_id=0, has_side_effects=True, vmem_limit_bytes=VMEM_LIMIT
        ),
    )(*args)
    return pl.pallas_call(
        write_out,
        out_shape=out_shape,
        in_specs=[hbm] * 7,
        out_specs=[hbm] * 7,
        scratch_shapes=[pltpu.VMEM(a.shape, a.dtype) for a in out_shape] + [dma((14,))],
        compiler_params=pltpu.CompilerParams(vmem_limit_bytes=VMEM_LIMIT),
    )(*results)


def solution(mesh):
    split = P("frame", "space", None)
    return jax.shard_map(
        shards,
        mesh=mesh,
        in_specs=(split,) * 7 + (P(),) * 4,
        out_specs=(split,) * 6 + (P(),),
        check_vma=False,
    )
```

```python
import functools

import functools

import jax
import jax.numpy as jnp
from jax import lax
from jax.experimental import pallas as pl
from jax.experimental.pallas import tpu as pltpu
from jax.sharding import PartitionSpec as P

F32, BF16 = jnp.float32, jnp.bfloat16
H = 16
HD = 96
NS = 32
NF = 16
FL = 2
PL = 64
SEQ = NS * PL
ROWS = PL * HD // 128
SPAN = 512
QB = 256
KT = 256
VMEM_LIMIT = 123 * 2**19
EARLY = 5
SCALE = HD**-0.5
LOG2E = 1.4426950408889634
NT = (((1,), (1,)), ((), ()))
NN = (((1,), (0,)), ((), ()))
MESH = pl.DeviceIdType.MESH


def mm(a, b, dims):
    return lax.dot_general(a, b, dims, preferred_element_type=F32)


def lanes(shape):
    return lax.broadcasted_iota(jnp.int32, shape, len(shape) - 1)


def split_heads(x):
    a, b, c = x[:, 0:128], x[:, 128:256], x[:, 256:384]
    lane = lanes(a.shape)
    return (
        a,
        jnp.where(lane < 32, pltpu.roll(a, 32, 1), pltpu.roll(b, 32, 1)),
        jnp.where(lane < 64, pltpu.roll(b, 64, 1), pltpu.roll(c, 64, 1)),
        pltpu.roll(c, 96, 1),
    )


def join_heads(w, x, y, z):
    lane = lanes(w.shape)
    x, y, z = pltpu.roll(x, 96, 1), pltpu.roll(y, 64, 1), pltpu.roll(z, 32, 1)
    return jnp.where(lane < 96, w, x), jnp.where(lane < 64, x, y), jnp.where(lane < 32, y, z)


def pack_tiles(t0, t1, t2, t3):
    lane = lanes(t0.shape)
    return (
        jnp.where(lane < 96, t0, pltpu.roll(t3, 96, 1)),
        jnp.where(lane < 96, t1, pltpu.roll(t3, 64, 1)),
        jnp.where(lane < 96, t2, pltpu.roll(t3, 32, 1)),
    )


def unpack_tiles(p0, p1, p2):
    lane = lanes(p0.shape)
    zero = jnp.zeros_like(p0)
    last = jnp.where(lane < 32, pltpu.roll(p0, 32, 1), pltpu.roll(p1, 64, 1))
    last = jnp.where(lane < 64, last, pltpu.roll(p2, 96, 1))
    return tuple(jnp.where(lane < 96, t, zero) for t in (p0, p1, p2, last))


def tiles_of(ref, lead, count=3):
    return [ref[(*lead, pl.ds(16 * t, 16), slice(None))] for t in range(count)]


def attend(q, ks, vs, g, kt, dq, dk, dv, s_scr, p_scr, span, masked):
    tiles = span // KT
    for c in range(SEQ // 128):
        kt[:, c * 128 : (c + 1) * 128] = ks[c * 128 : (c + 1) * 128, :].T
    dk[...] = jnp.zeros_like(dk)
    dv[...] = jnp.zeros_like(dv)

    def step(start, base):
        rows = pl.ds(pl.multiple_of(start, QB), QB)
        keys = [pl.ds(pl.multiple_of(base + t * KT, KT), KT) for t in range(tiles)]
        tile = [pl.ds(t * KT, KT) for t in range(tiles)]
        qi, gi = q[rows, :], g[rows, :]
        if masked:
            key_pos = lax.broadcasted_iota(jnp.int32, (KT, QB), 0) & 15
            same = key_pos == (lanes((KT, QB)) & 15)
        top = None
        for t in range(tiles):
            s = mm(ks[keys[t], :], qi, NT)
            if masked:
                s = jnp.where(same, s, -jnp.inf)
            s_scr[tile[t], :] = s
            here = jnp.max(s.reshape(KT // 8, 8, QB), axis=0)
            top = here if top is None else jnp.maximum(top, here)
        top = jnp.max(top, axis=0, keepdims=True)
        total = jnp.zeros((8, QB), F32)
        delta = jnp.zeros((8, QB), F32)
        for t in range(tiles):
            e = jnp.exp2((s_scr[tile[t], :] - top) * (SCALE * LOG2E))
            dp = mm(vs[keys[t], :], gi, NT)
            s_scr[tile[t], :] = e
            p_scr[tile[t], :] = dp
            total += jnp.sum(e.reshape(KT // 8, 8, QB), axis=0)
            delta += jnp.sum((e * dp).reshape(KT // 8, 8, QB), axis=0)
        inv = 1.0 / jnp.sum(total, axis=0, keepdims=True)
        delta = jnp.sum(delta, axis=0, keepdims=True) * inv
        dq_t = jnp.zeros((HD, QB), F32)
        for t in range(tiles):
            p = s_scr[tile[t], :] * inv
            ds = (p * (p_scr[tile[t], :] - delta) * SCALE).astype(BF16)
            dv[keys[t], :] += mm(p.astype(BF16), gi, NN)
            dk[keys[t], :] += mm(ds, qi, NN)
            dq_t += mm(kt[0:HD, keys[t]], ds, NN)
        dq[rows, 0:HD] = dq_t.T.astype(BF16)

    def outer(b, carry):
        for i in range(span // QB if masked else 1):
            step(b * (span if masked else QB) + i * QB, b * span if masked else 0)
        return carry

    lax.fori_loop(0, SEQ // (span if masked else QB), outer, 0)


def kernel(
    q_s_hbm, k_s_hbm, v_s_hbm, q_t_hbm, k_t_hbm, v_t_hbm, grad_hbm,
    gain_ks_hbm, gain_vs_hbm, gain_kt_hbm, gain_vt_hbm,
    dq_s_hbm, dk_s_hbm, dv_s_hbm, dq_t_hbm, dk_t_hbm, dv_t_hbm, ia3_hbm,
    q_s, k_s, v_s, q_t, k_t, v_t, grad, gain_ks, gain_vs, gain_kt, gain_vt, load_sem,
    dq_s, dk_s, dv_s, dq_t, dk_t, dv_t, ia3, store_sem,
    s_out, s_in, t_out, t_in, tg_out, tg_in, sb_out, sb_in, tb_out, tb_in,
    q, k, v, ks, vs, g, kt, dq, dk, dv, s_scr, p_scr, gains,
    a_out, a_out2, as1, at1, as2, at2,
    tg_sem, send_sem, s_sem, t_sem, sb_sem, tb_sem, a_send, as1_sem, at1_sem, as2_sem, at2_sem,
):
    f = lax.axis_index("frame")
    s = lax.axis_index("space")
    z, y = s // 4, s % 4
    fx, fz, fc = f // 4, (f // 2) % 2, f % 2
    half = s // 16
    s_set, s_fl, s_place = (half + fz) % 2, (s // 8) % 2, s % 8
    t_set, t_place = (fz + half) % 2, 2 * fx + fc

    def group_of_z(zi):
        return (zi // 2) % 2, 2 * ((zi // 4 + fz) % 2) + zi % 2

    def frame_of(hg, j):
        return 4 * (2 * (hg % 2) + j // 2) + 2 * ((hg // 2 + half) % 2) + j % 2

    def space_id(i):
        zi, yi = i // 4, i % 4
        zi_half = (z // 4 + 1 + zi // 4) % 2
        return (4 * zi_half + (z + zi) % 4) * 4 + (y + yi) % 4

    def space_z(i):
        zi_half = (z // 4 + 1 + i // 4) % 2
        return 4 * zi_half + (z + i) % 4

    def frame_id(i):
        zi = (fz + 1 + i // 8) % 2
        return 4 * ((fx + i // 2) % 4) + 2 * zi + (fc + i) % 2

    def send(axis, me, to, src, dst, ssem, rsem):
        @pl.when(to != me)
        def _():
            pltpu.make_async_remote_copy(
                src.at[to], dst.at[me], ssem, rsem.at[me], device_id={axis: to}, device_id_type=MESH
            ).start()

        @pl.when(to == me)
        def _():
            pltpu.make_async_copy(src.at[me], dst.at[me], rsem.at[me]).start()

    def arrived(dst, rsem, j):
        pltpu.make_async_copy(dst.at[j], dst.at[j], rsem.at[j]).wait()

    def sent(src, n, sem):
        part = src.at[pl.ds(0, n - 1)]
        pltpu.make_async_copy(part, part, sem).wait()

    def loop(n, body):
        def run(i, carry):
            body(i)
            return carry

        lax.fori_loop(0, n, run, 0)

    names = ("grad", "q_s", "k_s", "v_s", "q_t", "k_t", "v_t")
    loads = {}
    for n, (name, src, dst) in enumerate(
        zip(
            names + ("gain_ks", "gain_vs", "gain_kt", "gain_vt"),
            (grad_hbm, q_s_hbm, k_s_hbm, v_s_hbm, q_t_hbm, k_t_hbm, v_t_hbm)
            + (gain_ks_hbm, gain_vs_hbm, gain_kt_hbm, gain_vt_hbm),
            (grad, q_s, k_s, v_s, q_t, k_t, v_t, gain_ks, gain_vs, gain_kt, gain_vt),
        )
    ):
        loads[name] = pltpu.make_async_copy(src, dst, load_sem.at[n])
        loads[name].start()

    barrier = pltpu.get_barrier_semaphore()

    def greet(axis, me, n):
        def body(i):
            pl.semaphore_signal(
                barrier, inc=1, device_id={axis: (me + 1 + i) % n}, device_id_type=MESH
            )

        loop(n - 1, body)

    greet("space", s, NS)
    greet("frame", f, NF)

    def greet_items(i):
        at = {"frame": 4 * (i // 4) + 2 * (1 - fz) + (i // 2) % 2}
        at["space"] = 16 * (1 - half) + 8 * (i % 2) + t_place
        pl.semaphore_signal(barrier, inc=1, device_id=at, device_id_type=MESH)

    loop(16, greet_items)

    def pack_group(ref, fl, hg):
        cols = pl.ds(pl.multiple_of(hg * 384, 128), 384)
        heads = split_heads(ref[fl, :, cols])
        return [pack_tiles(*(x[16 * t : 16 * t + 16] for t in range(4))) for x in heads]

    def put(ref, lead, tiles):
        for t in range(3):
            ref[(*lead, pl.ds(16 * t, 16), slice(None))] = tiles[t]

    for name in names[:4]:
        loads[name].wait()
    pl.semaphore_wait(barrier, NS + NF - 2 + 16)

    def space_pack(i):
        zi = space_z(i)
        fl, hg = group_of_z(zi)
        for n, ref in enumerate((q_s, k_s, v_s, grad)):
            packed = pack_group(ref, fl, hg)
            for j in range(4):
                put(s_out, (4 * zi + j, n), packed[j])
        for j in range(4):
            send("space", s, 4 * zi + (y + j) % 4, s_out, s_in, send_sem.at[0], s_sem)

    loop(8, space_pack)

    for name in names[4:]:
        loads[name].wait()

    def time_pack(hg):
        for fl in range(FL):
            for n, ref in enumerate((q_t, k_t, v_t, grad)):
                packed = pack_group(ref, fl, hg)
                for j in range(4):
                    if n == 3:
                        put(tg_out, (frame_of(hg, j), fl), packed[j])
                    else:
                        put(t_out, (frame_of(hg, j), fl, n), packed[j])

    loop(4, time_pack)

    def time_send(i):
        send("frame", f, frame_id(i), t_out, t_in, send_sem.at[1], t_sem)

    def time_send_near(i):
        time_send(8 + i)
        send("frame", f, frame_id(8 + i), tg_out, tg_in, send_sem.at[4], tg_sem)

    loop(8, time_send)
    loop(8, time_send_near)

    for name in ("gain_ks", "gain_vs", "gain_kt", "gain_vt"):
        loads[name].wait()

    for i in range(H // 4):
        for r, ref in enumerate((gain_ks, gain_vs, gain_kt, gain_vt)):
            heads = split_heads(jnp.broadcast_to(ref[384 * i : 384 * i + 384].reshape(1, 384), (8, 384)))
            for j in range(4):
                gains[r, 4 * i + j] = heads[j]


    def unpack_item(leads, row_of, gain_k, gain_v):
        for n, dst in enumerate((q, k, v, g)):
            tiles = unpack_tiles(*tiles_of(*leads[n]))
            for t in range(4):
                rows = pl.ds(pl.multiple_of(row_of(t), 16), 16)
                dst[rows, :] = tiles[t]
                if n == 1:
                    ks[rows, :] = (tiles[t].astype(F32) * gain_k).astype(BF16)
                if n == 2:
                    vs[rows, :] = (tiles[t].astype(F32) * gain_v).astype(BF16)

    def pack_item(ref, lead, row_of, gain_k, gain_v):
        for n, src in enumerate((dq, dk, dv)):
            tiles = []
            for t in range(4):
                x = src[pl.ds(pl.multiple_of(row_of(t), 16), 16), :]
                if n:
                    gain = gain_k if n == 1 else gain_v
                    x = (x.astype(BF16).astype(F32) * gain).astype(BF16)
                tiles.append(x)
            put(ref, (*lead, n), pack_tiles(*tiles))

    def gain_rows(row, head):
        return gains[row, head, 0:1, :], gains[row + 1, head, 0:1, :]

    def terms(slot):
        def body(i, carry):
            rows = pl.ds(pl.multiple_of(i * 128, 128), 128)
            out = []
            for acc, a, b in ((carry[0], dk, k), (carry[1], dv, v)):
                prod = a[rows, :].astype(BF16).astype(F32) * b[rows, :].astype(F32)
                out.append(acc + jnp.sum(prod.reshape(16, 8, 128), axis=0))
            return tuple(out)

        zero = jnp.zeros((8, 128), F32)
        tk, tv = lax.fori_loop(0, SEQ // 128, body, (zero, zero))
        a_out[slot] = jnp.concatenate(
            [jnp.sum(tk, axis=0, keepdims=True), jnp.sum(tv, axis=0, keepdims=True)]
        )

    def share(axis, me, n, block, slot, dst, rsem):
        dst[me] = block[...]

        def body(i):
            pltpu.make_async_remote_copy(
                block,
                dst.at[me],
                a_send.at[slot],
                rsem.at[me],
                device_id={axis: (me + 1 + i) % n},
                device_id_type=MESH,
            ).start()

        loop(n - 1, body)

    def collect(me, n, dst, rsem):
        loop(n - 1, lambda i: arrived(dst, rsem, (me + 1 + i) % n))

    dq[...] = jnp.zeros_like(dq)

    gk_s, gv_s = gain_rows(0, 8 * s_set + s_place)

    def space_unpack(i):
        j = space_id(i)
        arrived(s_in, s_sem, j)
        unpack_item([(s_in, (j, n)) for n in range(4)], lambda t: PL * j + 16 * t, gk_s, gv_s)

    def space_unpack_far(i):
        space_unpack(i)
        j = space_id(i)
        at = {"frame": 4 * (s_place // 2) + 2 * (1 - fz) + s_place % 2, "space": j}
        pltpu.make_async_remote_copy(
            s_in.at[j, 3],
            tg_in.at[f, s_fl],
            send_sem.at[5],
            tg_sem.at[f],
            device_id=at,
            device_id_type=MESH,
        ).start()

    loop(NS // 2, space_unpack_far)
    loop(NS // 2, lambda i: space_unpack(NS // 2 + i))
    attend(q, ks, vs, g, kt, dq, dk, dv, s_scr, p_scr, SEQ, False)
    terms(0)
    share("frame", f, NF, a_out.at[0], 0, as1, as1_sem)

    def space_back(i):
        j = space_id(i)
        pack_item(sb_out, (j,), lambda t: PL * j + 16 * t, gk_s, gv_s)
        send("space", s, j, sb_out, sb_in, send_sem.at[2], sb_sem)

    loop(NS, space_back)

    gk_t, gv_t = gain_rows(2, 8 * t_set + t_place)

    def time_row(j, fl):
        return lambda t: SPAN * t + 16 * (FL * j + fl)

    def time_unpack(i):
        j = frame_id(i)
        arrived(t_in, t_sem, j)
        arrived(tg_in, tg_sem, j)
        for fl in range(FL):
            leads = [(t_in, (j, fl, n)) for n in range(3)] + [(tg_in, (j, fl))]
            unpack_item(leads, time_row(j, fl), gk_t, gv_t)

    loop(NF, time_unpack)
    collect(f, NF, as1, as1_sem)
    for r in range(2):
        parts = [as1[4 * x + 2 * r + c] for x in range(4) for c in range(2)]
        a_out2[0, 2 * r : 2 * r + 2, :] = functools.reduce(jnp.add, parts)
    share("space", s, NS, a_out2.at[0], 2, as2, as2_sem)
    attend(q, ks, vs, g, kt, dq, dk, dv, s_scr, p_scr, SPAN, True)
    terms(1)
    share("space", s, NS, a_out.at[1], 1, at1, at1_sem)

    def time_back(i):
        j = frame_id(i)
        for fl in range(FL):
            pack_item(tb_out, (j, fl), time_row(j, fl), gk_t, gv_t)
        send("frame", f, j, tb_out, tb_in, send_sem.at[3], tb_sem)

    loop(EARLY, time_back)

    def unpack_group(ref, leads, dst, fl, hg):
        heads = [unpack_tiles(*tiles_of(ref, lead)) for lead in leads]
        for t in range(4):
            pieces = join_heads(*(h[t] for h in heads))
            for c in range(3):
                cols = pl.ds(pl.multiple_of(hg * 384 + c * 128, 128), 128)
                dst[fl, pl.ds(16 * t, 16), cols] = pieces[c]

    stores = []

    def store(src, dst):
        copy = pltpu.make_async_copy(src, dst, store_sem.at[len(stores)])
        copy.start()
        stores.append(copy)

    def space_home(i):
        zi = space_z(i)
        for j in range(4):
            arrived(sb_in, sb_sem, 4 * zi + j)
        fl, hg = group_of_z(zi)
        for n, dst in enumerate((dq_s, dk_s, dv_s)):
            unpack_group(sb_in, [(4 * zi + j, n) for j in range(4)], dst, fl, hg)

    loop(8, space_home)
    for src, dst in ((dq_s, dq_s_hbm), (dk_s, dk_s_hbm), (dv_s, dv_s_hbm)):
        store(src, dst)
    collect(s, NS, at1, at1_sem)
    for b in range(2):
        a_out2[1, 2 * b : 2 * b + 2, :] = jnp.sum(at1[16 * b : 16 * b + 16], axis=0)
    share("frame", f, NF, a_out2.at[1], 3, at2, at2_sem)
    loop(NF - EARLY, lambda i: time_back(EARLY + i))
    collect(s, NS, as2, as2_sem)

    def time_home(hg):
        for j in range(4):
            arrived(tb_in, tb_sem, frame_of(hg, j))
        for fl in range(FL):
            for n, dst in enumerate((dq_t, dk_t, dv_t)):
                unpack_group(tb_in, [(frame_of(hg, j), fl, n) for j in range(4)], dst, fl, hg)

    loop(H // 4, time_home)
    for src, dst in ((dq_t, dq_t_hbm), (dk_t, dk_t_hbm), (dv_t, dv_t_hbm)):
        store(src, dst)

    norm = float(SEQ * NF * FL) ** -0.5
    collect(f, NF, at2, at2_sem)
    for hg in range(H // 4):
        e, space, time = hg // 2, [], []
        for j in range(4):
            place = 4 * (hg % 2) + j
            here, there = 16 * e + place, 16 * (1 - e) + place
            space.append(
                (as2[here, 0:2, :] + as2[here + 8, 0:2, :])
                + (as2[there, 2:4, :] + as2[there + 8, 2:4, :])
            )
            peer = 4 * (place // 2) + place % 2
            time.append(at2[peer + 2 * e, 0:2, :] + at2[peer + 2 * (1 - e), 2:4, :])
        for row, heads in ((0, space), (2, time)):
            for c, piece in enumerate(join_heads(*heads)):
                col = hg * 384 + c * 128
                ia3[row : row + 2, col : col + 128] = piece * norm
    store(ia3, ia3_hbm)

    sent(s_out, NS, send_sem.at[0])
    sent(t_out, NF, send_sem.at[1])
    sent(tg_out, 8, send_sem.at[4])
    sent(tg_in, 9, send_sem.at[5])
    sent(sb_out, NS, send_sem.at[2])
    sent(tb_out, NF, send_sem.at[3])
    sent(as1, NF, a_send.at[0])
    sent(at1, NS, a_send.at[1])
    sent(as2, NS, a_send.at[2])
    sent(at2, NF, a_send.at[3])
    for copy in stores:
        copy.wait()


def write_out(*refs):
    n = len(refs) // 3
    sems = refs[-1]
    loads = [pltpu.make_async_copy(refs[i], refs[2 * n + i], sems.at[i]) for i in range(n)]
    stores = [pltpu.make_async_copy(refs[2 * n + i], refs[n + i], sems.at[n + i]) for i in range(n)]
    for load in loads:
        load.start()
    for load, store in zip(loads, stores):
        load.wait()
        store.start()
    for store in stores:
        store.wait()


def shards(*args):
    full = jax.ShapeDtypeStruct((FL, PL, H * HD), BF16)
    hbm = pl.BlockSpec(memory_space=pltpu.HBM)

    def nat(dtype):
        return pltpu.VMEM((SEQ, 128), dtype)

    dma = pltpu.SemaphoreType.DMA
    scratch = [
        *[pltpu.VMEM((FL, PL, H * HD), BF16) for _ in range(7)],
        *[pltpu.VMEM((H * HD,), F32) for _ in range(4)],
        dma((11,)),
        *[pltpu.VMEM((FL, PL, H * HD), BF16) for _ in range(6)],
        pltpu.VMEM((4, H * HD), F32),
        dma((7,)),
        pltpu.VMEM((NS, 4, ROWS, 128), BF16),
        pltpu.VMEM((NS, 4, ROWS, 128), BF16),
        pltpu.VMEM((NF, FL, 3, ROWS, 128), BF16),
        pltpu.VMEM((NF, FL, 3, ROWS, 128), BF16),
        pltpu.VMEM((NF, FL, ROWS, 128), BF16),
        pltpu.VMEM((NF, FL, ROWS, 128), BF16),
        pltpu.VMEM((NS, 3, ROWS, 128), BF16),
        pltpu.VMEM((NS, 3, ROWS, 128), BF16),
        pltpu.VMEM((NF, FL, 3, ROWS, 128), BF16),
        pltpu.VMEM((NF, FL, 3, ROWS, 128), BF16),
        *[nat(BF16) for _ in range(6)],
        pltpu.VMEM((128, SEQ), BF16),
        nat(BF16),
        nat(F32),
        nat(F32),
        pltpu.VMEM((SEQ, QB), F32),
        pltpu.VMEM((SEQ, QB), F32),
        pltpu.VMEM((4, H, 8, 128), F32),
        *[pltpu.VMEM((n, r, 128), F32) for n, r in ((2, 2), (2, 4), (NF, 2), (NS, 2), (NS, 4), (NF, 4))],
        dma((NF,)),
        dma((6,)),
        dma((NS,)),
        dma((NF,)),
        dma((NS,)),
        dma((NF,)),
        dma((4,)),
        dma((NF,)),
        dma((NS,)),
        dma((NS,)),
        dma((NF,)),
    ]
    out_shape = [full] * 6 + [jax.ShapeDtypeStruct((4, H * HD), F32)]
    results = pl.pallas_call(
        kernel,
        out_shape=out_shape,
        in_specs=[hbm] * 11,
        out_specs=[hbm] * 7,
        scratch_shapes=scratch,
        compiler_params=pltpu.CompilerParams(
            collective_id=0, has_side_effects=True, vmem_limit_bytes=VMEM_LIMIT
        ),
    )(*args)
    return pl.pallas_call(
        write_out,
        out_shape=out_shape,
        in_specs=[hbm] * 7,
        out_specs=[hbm] * 7,
        scratch_shapes=[pltpu.VMEM(a.shape, a.dtype) for a in out_shape] + [dma((14,))],
        compiler_params=pltpu.CompilerParams(vmem_limit_bytes=VMEM_LIMIT),
    )(*results)


def solution(mesh):
    split = P("frame", "space", None)
    return jax.shard_map(
        shards,
        mesh=mesh,
        in_specs=(split,) * 7 + (P(),) * 4,
        out_specs=(split,) * 6 + (P(),),
        check_vma=False,
    )
```
